512 devices in a mesh: rep: 64 (over z_lo, x, core), tp: 8 (over z_hi, y).
Axes of the slice: x: 4, y: 4, z: 16 (z_hi: 2, z_lo: 8; z = z_hi * 8 + z_lo), core: 2. Of those that a mesh axis runs over, the one named last changes fastest.
Arguments:
- steps_done: int32 [1], replicated, may hold values from 1000 to 99999
- gate_weight: bfloat16 [64, 704, 2048], P('rep', 'tp'), may hold values from -3 to 3
- up_weight: bfloat16 [64, 704, 2048], P('rep', 'tp'), may hold values from -3 to 3
- down_weight: bfloat16 [64, 704, 2048], P('rep', 'tp'), may hold values from -3 to 3
- gate_momentum: bfloat16 [64, 704, 2048], P('rep', 'tp'), may hold values from -0.099609375 to 0.099609375
- up_momentum: bfloat16 [64, 704, 2048], P('rep', 'tp'), may hold values from -0.099609375 to 0.099609375
- down_momentum: bfloat16 [64, 704, 2048], P('rep', 'tp'), may hold values from -0.099609375 to 0.099609375
- gate_variance: bfloat16 [64, 704, 2048], P('rep', 'tp'), may hold values from 0.0009994507 to 0.0099487305
- up_variance: bfloat16 [64, 704, 2048], P('rep', 'tp'), may hold values from 0.0009994507 to 0.0099487305
- down_variance: bfloat16 [64, 704, 2048], P('rep', 'tp'), may hold values from 0.0009994507 to 0.0099487305
- inputs: bfloat16 [2, 8192, 2048], P(None, 'rep', 'tp'), may hold values from -6 to 6
- cotangent: bfloat16 [2, 8192, 2048], P(None, 'rep', 'tp'), may hold values from -6 to 6
Outputs:
- gate_result: bfloat16 [64, 704, 2048], P('rep', 'tp')
- up_result: bfloat16 [64, 704, 2048], P('rep', 'tp')
- down_result: bfloat16 [64, 704, 2048], P('rep', 'tp')
The draws below stay inside these ranges and needn't reach their ends.
All inputs are finite; a program needn't handle non-finite values.
Results may differ from the reference program's by a relative error of at most 0.014.
Values may be sent and summed in bfloat16 or wider, within the bound.
No kernel may reach another device: no remote copies, remote signals or barrier semaphores. Data moves between devices by JAX's collectives and lax.ppermute only.
A program may use at most 128 MiB of HBM per device.

```python
import math
import jax
import jax.numpy as jnp
from jax import lax

D = 2048
FF = 5632
SPAN = 8
STEPS = 2
TOK = 1024
REPLICAS = 8
ROWS = 8192


def level_of(stream_key, shape, split, smallest, high):
    level = 1.0
    for axis_at, blocks in split:
        heights = jax.random.uniform(jax.random.fold_in(jax.random.fold_in(stream_key, 6), axis_at), (blocks,), jnp.float32, smallest / len(split), high / len(split))
        level = level * jnp.repeat(jnp.exp(heights), shape[axis_at] // blocks).reshape((-1,) + (1,) * (len(shape) - 1 - axis_at))
    return level


def scatter_about(own_key, shape, spread, most, shards=(), dtype=jnp.bfloat16):
    gain = level_of(own_key, shape, shards, -0.22, 0.18) if shards else 1.0
    result = jax.random.normal(own_key, shape, jnp.float32) * spread * gain
    return jnp.minimum(jnp.maximum(result, -most), most).astype(dtype)


def setup_inputs(seed: int = 0) -> dict:
    streams_of = jax.random.split(jax.random.key(seed), 13)
    return {
        "steps_done": jax.random.randint(streams_of[0], (1,), 1000, 100000).astype(jnp.int32),
        "gate_weight": scatter_about(streams_of[1], (REPLICAS * SPAN, FF // SPAN, D), 0.5, 3.0, ((0, 64), (1, 8))),
        "up_weight": scatter_about(streams_of[2], (REPLICAS * SPAN, FF // SPAN, D), 0.5, 3.0, ((0, 64), (1, 8))),
        "down_weight": scatter_about(streams_of[3], (REPLICAS * SPAN, FF // SPAN, D), 0.5, 3.0, ((0, 64), (1, 8))),
        "gate_momentum": scatter_about(streams_of[4], (REPLICAS * SPAN, FF // SPAN, D), 0.02, 0.099609375, ((0, 64), (1, 8))),
        "up_momentum": scatter_about(streams_of[5], (REPLICAS * SPAN, FF // SPAN, D), 0.02, 0.099609375, ((0, 64), (1, 8))),
        "down_momentum": scatter_about(streams_of[6], (REPLICAS * SPAN, FF // SPAN, D), 0.02, 0.099609375, ((0, 64), (1, 8))),
        "gate_variance": jnp.clip(jnp.exp(math.log(0.0099487305) - 2.2979944 * jax.random.uniform(streams_of[7], (REPLICAS * SPAN, FF // SPAN, D), jnp.float32) ** level_of(streams_of[7], (REPLICAS * SPAN, FF // SPAN, D), ((0, 64), (1, 8)), -0.2, 0.2)), 0.0009994507, 0.0099487305).astype(jnp.bfloat16),
        "up_variance": jnp.clip(jnp.exp(math.log(0.0099487305) - 2.2979944 * jax.random.uniform(streams_of[8], (REPLICAS * SPAN, FF // SPAN, D), jnp.float32) ** level_of(streams_of[8], (REPLICAS * SPAN, FF // SPAN, D), ((0, 64), (1, 8)), -0.2, 0.2)), 0.0009994507, 0.0099487305).astype(jnp.bfloat16),
        "down_variance": jnp.clip(jnp.exp(math.log(0.0099487305) - 2.2979944 * jax.random.uniform(streams_of[9], (REPLICAS * SPAN, FF // SPAN, D), jnp.float32) ** level_of(streams_of[9], (REPLICAS * SPAN, FF // SPAN, D), ((0, 64), (1, 8)), -0.2, 0.2)), 0.0009994507, 0.0099487305).astype(jnp.bfloat16),
        "inputs": scatter_about(streams_of[10], (STEPS, ROWS, D), 1.0, 6.0, ((1, 64), (2, 8))),
        "cotangent": scatter_about(streams_of[11], (STEPS, ROWS, D), 1.0, 6.0, ((1, 64), (2, 8))),
    }


rate = 0.2
beta_one = 0.9
beta_two = 0.95
adam_eps = 1e-08
hop_levels = 5

def contract(left, right, left_dim, right_dim):
    return lax.dot_general(left, right, (((left_dim,), (right_dim,)), ((), ())), preferred_element_type=jnp.float32)

def adam_update(weight, grad, first, second, count):
    first = beta_one * first + (1.0 - beta_one) * grad
    second = beta_two * second + (1.0 - beta_two) * grad * grad
    fix_one = 1.0 - jnp.power(jnp.float32(beta_one), count)
    fix_two = 1.0 - jnp.power(jnp.float32(beta_two), count)
    step_size = rate * (first / fix_one) / (jnp.sqrt(second / fix_two) + adam_eps)
    return ((weight.astype(jnp.float32) - step_size).astype(jnp.bfloat16), first, second)

def local_step(weights, firsts, seconds, rows, grads_out, count):
    gate_w, up_w, down_w = weights
    inv_model = 1.0 / math.sqrt(D)
    inv_hidden = 1.0 / math.sqrt(FF)
    gate = contract(gate_w, rows, 1, 1) * inv_model
    upper = contract(up_w, rows, 1, 1) * inv_model
    sigma = jax.nn.sigmoid(gate)
    hidden = (gate * sigma * upper).astype(jnp.bfloat16)
    back = contract(down_w, grads_out, 1, 1) * inv_hidden
    grad_down = contract(hidden, grads_out, 1, 0) * inv_hidden
    d_gate = (back * upper * sigma * (1.0 + gate * (1.0 - sigma))).astype(jnp.bfloat16)
    d_up = (back * gate * sigma).astype(jnp.bfloat16)
    grad_gate = contract(d_gate, rows, 1, 0) * inv_model
    grad_up = contract(d_up, rows, 1, 0) * inv_model
    new_gate = adam_update(gate_w, grad_gate, firsts[0], seconds[0], count)
    new_up = adam_update(up_w, grad_up, firsts[1], seconds[1], count)
    new_down = adam_update(down_w, grad_down, firsts[2], seconds[2], count)
    outs = (new_gate, new_up, new_down)
    return (tuple((o[0] for o in outs)), tuple((o[1] for o in outs)), tuple((o[2] for o in outs)))

def blend(mine, peer):
    return ((mine.astype(jnp.float32) + peer.astype(jnp.float32)) * 0.5).astype(jnp.bfloat16)

def reference(steps_done, gate_weight, up_weight, down_weight, gate_momentum, up_momentum, down_momentum, gate_variance, up_variance, down_variance, inputs, cotangent):
    shape = (REPLICAS, FF, D)
    weights = tuple((w.reshape(shape) for w in (gate_weight, up_weight, down_weight)))
    firsts = tuple((m.reshape(shape).astype(jnp.float32) for m in (gate_momentum, up_momentum, down_momentum)))
    seconds = tuple((v.reshape(shape).astype(jnp.float32) for v in (gate_variance, up_variance, down_variance)))
    all_rows = inputs.reshape(STEPS, REPLICAS, TOK, D)
    all_grads = cotangent.reshape(STEPS, REPLICAS, TOK, D)
    for step in range(STEPS):
        count = (steps_done[0] + step + 1).astype(jnp.float32)

        def one_replica(packed):
            return local_step(packed[0], packed[1], packed[2], packed[3], packed[4], count)
        weights, firsts, seconds = lax.map(one_replica, (weights, firsts, seconds, all_rows[step], all_grads[step]))
        level = ((steps_done[0] + step) % hop_levels).astype(jnp.int32)
        offset = jnp.left_shift(jnp.int32(1), level) % REPLICAS
        weights = tuple((blend(w, jnp.roll(w, -offset, axis=0)) for w in weights))
    final = tuple((w.reshape(REPLICAS * SPAN, FF // SPAN, D) for w in weights))
    return (final[0], final[1], final[2])
```

```python
import math

import jax
import jax.numpy as jnp
from jax import lax
from jax.experimental import pallas as pl
from jax.experimental.pallas import tpu as pltpu
from jax.sharding import Mesh, PartitionSpec as P

D = 2048
FF = 5632
STEPS = 2
ROWS = 88
PAD = 96
BLK = 256
TOKB = 128
TOK = 1024
NB = D // BLK

rate = 0.2
beta_one = 0.9
beta_two = 0.95
adam_eps = 1e-08
hop_levels = 5
INV_MODEL = 1.0 / math.sqrt(D)
INV_HIDDEN = 1.0 / math.sqrt(FF)


def dot(left, right, right_dim):
    return lax.dot_general(
        left, right, (((1,), (right_dim,)), ((), ())), preferred_element_type=jnp.float32
    )


def pad_rows(value):
    value = value.astype(jnp.float32)
    return jnp.concatenate(
        [value, jnp.zeros((PAD - ROWS, value.shape[1]), jnp.float32)], 0
    ).astype(jnp.bfloat16)


def step_kernel(step, fix, *refs):
    blended = step > 0
    weights, refs = refs[:3], refs[3:]
    if blended:
        peers, refs = refs[:3], refs[3:]
    firsts, seconds, gathered = refs[:3], refs[3:6], refs[6]
    refs = refs[7:]
    new_w, refs = refs[0], refs[1:]
    if not blended:
        new_m, new_v, refs = refs[0], refs[1], refs[2:]
    x_buf, c_buf, gu_buf, v_buf, d_buf, h_buf, sem = refs

    def fetch(kind, buf):
        copies = []
        for t in range(TOK // TOKB):
            for y in range(NB // 2):
                for z in range(2):
                    copies.append(
                        pltpu.make_async_copy(
                            gathered.at[t * (NB // 2) + y, step, kind, z],
                            buf.at[z * (NB // 2) + y, pl.ds(t * TOKB, TOKB), :],
                            sem.at[kind],
                        )
                    )
        return copies

    x_copies, c_copies = fetch(0, x_buf), fetch(1, c_buf)
    for copy in x_copies:
        copy.start()
    for copy in c_copies:
        copy.start()

    def weight(i, cols):
        mine = weights[i][:, cols].astype(jnp.float32)
        if blended:
            mine = ((mine + peers[i][:, cols].astype(jnp.float32)) * 0.5)
            mine = mine.astype(jnp.bfloat16).astype(jnp.float32)
        return mine

    def prepare(j, _):
        cols = pl.ds(pl.multiple_of(j * BLK, BLK), BLK)
        gu_buf[0:PAD, cols] = pad_rows(weight(0, cols))
        gu_buf[PAD : 2 * PAD, cols] = pad_rows(weight(1, cols))
        v_buf[:, cols] = pad_rows(weight(2, cols))
        return 0

    lax.fori_loop(0, NB, prepare, 0)
    for copy in x_copies:
        copy.wait()
    for copy in c_copies:
        copy.wait()

    def forward(t, _):
        toks = pl.ds(pl.multiple_of(t * 256, 256), 256)
        gu = jnp.zeros((2 * PAD, 256), jnp.float32)
        back = jnp.zeros((PAD, 256), jnp.float32)
        for j in range(NB):
            cols = slice(j * BLK, (j + 1) * BLK)
            gu += dot(gu_buf[:, cols], x_buf[j, toks, :], 1)
        for j in range(NB):
            cols = slice(j * BLK, (j + 1) * BLK)
            back += dot(v_buf[:, cols], c_buf[j, toks, :], 1)
        gate, upper = gu[:PAD] * INV_MODEL, gu[PAD:] * INV_MODEL
        back = back * INV_HIDDEN
        sigma = jax.nn.sigmoid(gate)
        gs = gate * sigma
        h_buf[:, toks] = (gs * upper).astype(jnp.bfloat16)
        d_gate = back * upper * sigma * (1.0 + gate * (1.0 - sigma))
        d_buf[0:PAD, toks] = d_gate.astype(jnp.bfloat16)
        d_buf[PAD : 2 * PAD, toks] = (back * gs).astype(jnp.bfloat16)
        return 0

    lax.fori_loop(0, TOK // 256, forward, 0)
    rate_one, inv_two = fix[0], fix[1]

    def backward(j, _):
        cols = pl.ds(pl.multiple_of(j * BLK, BLK), BLK)
        gu = dot(d_buf[...], x_buf[j], 0) * INV_MODEL
        down = dot(h_buf[...], c_buf[j], 0) * INV_HIDDEN
        for i, grad in enumerate((gu[:ROWS], gu[PAD : PAD + ROWS], down[:ROWS])):
            first = firsts[i][:, cols].astype(jnp.float32)
            second = seconds[i][:, cols].astype(jnp.float32)
            first = beta_one * first + (1.0 - beta_one) * grad
            second = beta_two * second + (1.0 - beta_two) * grad * grad
            change = (first * rate_one) / (jnp.sqrt(second * inv_two) + adam_eps)
            new_w[i, :, cols] = (weight(i, cols) - change).astype(jnp.bfloat16)
            if not blended:
                new_m[i, :, cols] = first
                new_v[i, :, cols] = second
        return 0

    lax.fori_loop(0, NB, backward, 0)


def run_step(step, fix, weights, peers, firsts, seconds, gathered):
    vmem = pl.BlockSpec(memory_space=pltpu.VMEM)
    args = [*weights, *(peers if step else ()), *firsts, *seconds]
    shape = (3, ROWS, D)
    outs = [jax.ShapeDtypeStruct(shape, jnp.bfloat16)]
    if not step:
        outs += [jax.ShapeDtypeStruct(shape, jnp.float32)] * 2
    mults = 6 * ROWS * TOK * D

    def body(*refs):
        step_kernel(step, *refs)

    return pl.pallas_call(
        body,
        out_shape=outs,
        in_specs=[pl.BlockSpec(memory_space=pltpu.SMEM)]
        + [vmem] * len(args)
        + [pl.BlockSpec(memory_space=pl.ANY)],
        out_specs=[vmem] * len(outs),
        scratch_shapes=[
            pltpu.VMEM((NB, TOK, BLK), jnp.bfloat16),
            pltpu.VMEM((NB, TOK, BLK), jnp.bfloat16),
            pltpu.VMEM((2 * PAD, D), jnp.bfloat16),
            pltpu.VMEM((PAD, D), jnp.bfloat16),
            pltpu.VMEM((2 * PAD, TOK), jnp.bfloat16),
            pltpu.VMEM((PAD, TOK), jnp.bfloat16),
            pltpu.SemaphoreType.DMA((2,)),
        ],
        compiler_params=pltpu.CompilerParams(vmem_limit_bytes=48 * 2**20),
        cost_estimate=pl.CostEstimate(
            flops=2 * mults, bytes_accessed=16 * 2**20, transcendentals=ROWS * TOK
        ),
        name="adam_step",
    )(fix, *args, gathered)


def shift_rep(value, hops):
    return lax.ppermute(value, "zl", [((i + hops) % 8, i) for i in range(8)])


def exchange(value, level):
    branches = [lambda v, h=2**p % 8: shift_rep(v, h) if h else v for p in range(hop_levels)]
    return lax.switch(level, branches, value)


def local(steps_done, *arrays):
    weights = [a[0] for a in arrays[0:3]]
    firsts = [a[0] for a in arrays[3:6]]
    seconds = [a[0] for a in arrays[6:9]]
    inputs, cotangent = arrays[9:]
    own = jnp.stack([inputs, cotangent], 1)
    other = lax.ppermute(own, "zh", [(0, 1), (1, 0)])
    low = lax.axis_index("zh") == 0
    both = jnp.stack([jnp.where(low, own, other), jnp.where(low, other, own)], 2)
    gathered = lax.all_gather(both, ("x", "c", "y"), axis=0)
    peers = None
    for step in range(STEPS):
        count = (steps_done[0] + step + 1).astype(jnp.float32)
        level = (steps_done[0] + step) % hop_levels
        fix_one = 1.0 - jnp.power(jnp.float32(beta_one), count)
        fix_two = 1.0 - jnp.power(jnp.float32(beta_two), count)
        fix = jnp.stack([rate / fix_one, 1.0 / fix_two])
        new = run_step(step, fix, weights, peers, firsts, seconds, gathered)
        peer = exchange(new[0], level)
        weights = [new[0][i] for i in range(3)]
        peers = [peer[i] for i in range(3)]
        if step == 0:
            firsts, seconds = [new[1][i] for i in range(3)], [new[2][i] for i in range(3)]
    return tuple(
        ((w.astype(jnp.float32) + p.astype(jnp.float32)) * 0.5).astype(jnp.bfloat16)[None]
        for w, p in zip(weights, peers)
    )


def solution(mesh):
    fine = Mesh(mesh.devices.reshape(8, 4, 2, 2, 4), ("zl", "x", "c", "zh", "y"))
    rep, tp = ("zl", "x", "c"), ("zh", "y")
    weight = P(rep, tp, None)
    return jax.shard_map(
        local,
        mesh=fine,
        in_specs=(P(),) + (weight,) * 9 + (P(None, rep, tp),) * 2,
        out_specs=(weight,) * 3,
        check_vma=False,
    )
```

```python
import math

import jax
import jax.numpy as jnp
from jax import lax
from jax.experimental import pallas as pl
from jax.experimental.pallas import tpu as pltpu
from jax.sharding import Mesh, PartitionSpec as P

D = 2048
FF = 5632
STEPS = 2
ROWS = 88
PAD = 96
BLK = 256
TOKB = 128
TOK = 1024
NB = D // BLK

rate = 0.2
beta_one = 0.9
beta_two = 0.95
adam_eps = 1e-08
hop_levels = 5
INV_MODEL = 1.0 / math.sqrt(D)
INV_HIDDEN = 1.0 / math.sqrt(FF)


def dot(left, right, right_dim):
    return lax.dot_general(
        left, right, (((1,), (right_dim,)), ((), ())), preferred_element_type=jnp.float32
    )


def pad_rows(value):
    value = value.astype(jnp.float32)
    return jnp.concatenate(
        [value, jnp.zeros((PAD - ROWS, value.shape[1]), jnp.float32)], 0
    ).astype(jnp.bfloat16)


def step_kernel(step, blended, pos, fix, *refs):
    weights, refs = refs[:3], refs[3:]
    if blended:
        peers, refs = refs[:3], refs[3:]
    firsts_in, seconds_in, refs = refs[:3], refs[3:6], refs[6:]
    mine, theirs, refs = refs[0], refs[1], refs[2:]
    new_w, refs = refs[:3], refs[3:]
    if not step:
        m_out, v_out, refs = refs[:3], refs[3:6], refs[6:]
    gu_buf, v_buf, d_buf, h_buf, w_buf, refs = *refs[:5], refs[5:]
    if blended:
        p_buf, refs = refs[0], refs[1:]
    m_buf, s_buf, refs = refs[0], refs[1], refs[2:]
    if not step:
        new_m, new_v, refs = refs[0], refs[1], refs[2:]
    sem, out_sem = refs
    core, high = pos[0], pos[1]

    def block(x, y, z, kind):
        parts = []
        for half, source in enumerate((mine, theirs)):
            from_core = core if half == 0 else 1 - core
            near = jnp.where(from_core == 0, x, y)
            far = jnp.where(from_core == 0, y, x)
            parts.append(source[far, near, jnp.where(high == z, 0, 1), kind])
        return jnp.concatenate(parts, 0)

    def whole(sources, buf, which):
        return [
            pltpu.make_async_copy(source, buf.at[i], sem.at[which])
            for i, source in enumerate(sources)
        ]

    tensors = whole(weights, w_buf, 0) + (whole(peers, p_buf, 0) if blended else [])
    moments = whole(firsts_in, m_buf, 1) + whole(seconds_in, s_buf, 1)
    for copy in tensors:
        copy.start()
    for copy in moments:
        copy.start()
    for copy in tensors:
        copy.wait()

    def weight(i, cols):
        mine = w_buf[i, :, cols].astype(jnp.float32)
        if blended:
            mine = (mine + p_buf[i, :, cols].astype(jnp.float32)) * 0.5
            mine = mine.astype(jnp.bfloat16).astype(jnp.float32)
        return mine

    def prepare(j, _):
        cols = pl.ds(pl.multiple_of(j * BLK, BLK), BLK)
        gu_buf[0:PAD, cols] = pad_rows(weight(0, cols))
        gu_buf[PAD : 2 * PAD, cols] = pad_rows(weight(1, cols))
        v_buf[:, cols] = pad_rows(weight(2, cols))
        return 0

    lax.fori_loop(0, NB, prepare, 0)

    def forward(t, _):
        toks = pl.ds(pl.multiple_of(t * 256, 256), 256)
        gu = jnp.zeros((2 * PAD, 256), jnp.float32)
        back = jnp.zeros((PAD, 256), jnp.float32)
        for j in range(NB):
            cols = slice(j * BLK, (j + 1) * BLK)
            gu += dot(gu_buf[:, cols], block(t, j % 4, j // 4, 0), 1)
        for j in range(NB):
            cols = slice(j * BLK, (j + 1) * BLK)
            back += dot(v_buf[:, cols], block(t, j % 4, j // 4, 1), 1)
        gate, upper = gu[:PAD] * INV_MODEL, gu[PAD:] * INV_MODEL
        back = back * INV_HIDDEN
        sigma = jax.nn.sigmoid(gate)
        gs = gate * sigma
        h_buf[:, toks] = (gs * upper).astype(jnp.bfloat16)
        d_gate = back * upper * sigma * (1.0 + gate * (1.0 - sigma))
        d_buf[0:PAD, toks] = d_gate.astype(jnp.bfloat16)
        d_buf[PAD : 2 * PAD, toks] = (back * gs).astype(jnp.bfloat16)
        return 0

    lax.fori_loop(0, TOK // 256, forward, 0)
    rate_one, inv_two = fix[0], fix[1]
    for copy in moments:
        copy.wait()

    def backward(j, _):
        cols = pl.ds(pl.multiple_of(j * BLK, BLK), BLK)
        y, z = j % 4, j // 4
        gu = jnp.zeros((2 * PAD, BLK), jnp.float32)
        down = jnp.zeros((PAD, BLK), jnp.float32)
        for x in range(4):
            toks = slice(x * 256, (x + 1) * 256)
            gu += dot(d_buf[:, toks], block(x, y, z, 0), 0)
            down += dot(h_buf[:, toks], block(x, y, z, 1), 0)
        gu, down = gu * INV_MODEL, down * INV_HIDDEN
        for i, grad in enumerate((gu[:ROWS], gu[PAD : PAD + ROWS], down[:ROWS])):
            first = m_buf[i, :, cols].astype(jnp.float32)
            second = s_buf[i, :, cols].astype(jnp.float32)
            first = beta_one * first + (1.0 - beta_one) * grad
            second = beta_two * second + (1.0 - beta_two) * grad * grad
            change = (first * rate_one) / (jnp.sqrt(second * inv_two) + adam_eps)
            new_w[i][:, cols] = (weight(i, cols) - change).astype(jnp.bfloat16)
            if not step:
                new_m[i, :, cols] = first
                new_v[i, :, cols] = second
                for buf, out in ((new_m, m_out), (new_v, v_out)):
                    pltpu.make_async_copy(
                        buf.at[i, :, cols], out[i].at[:, cols], out_sem
                    ).start()
        return 0

    lax.fori_loop(0, NB, backward, 0)
    if not step:
        for i in range(3):
            for buf, out in ((new_m, m_out), (new_v, v_out)):
                pltpu.make_async_copy(buf.at[i], out[i], out_sem).wait()


def run_step(step, pos, fix, weights, peers, firsts, seconds, gathered):
    smem = pl.BlockSpec(memory_space=pltpu.SMEM)
    vmem = pl.BlockSpec(memory_space=pltpu.VMEM)
    hbm = pl.BlockSpec(memory_space=pltpu.HBM)
    blended = peers is not None
    args = [*weights, *(peers or ()), *firsts, *seconds, *gathered]
    outs = [jax.ShapeDtypeStruct((ROWS, D), jnp.bfloat16)] * 3
    if not step:
        outs += [jax.ShapeDtypeStruct((ROWS, D), jnp.float32)] * 6
    mults = 6 * ROWS * TOK * D
    trio = (3, ROWS, D)

    def body(*refs):
        step_kernel(step, blended, *refs)

    new = pl.pallas_call(
        body,
        out_shape=outs,
        in_specs=[smem, smem] + [hbm] * (len(args) - 2) + [vmem] * 2,
        out_specs=[vmem] * 3 + [hbm] * (len(outs) - 3),
        scratch_shapes=[
            pltpu.VMEM((2 * PAD, D), jnp.bfloat16),
            pltpu.VMEM((PAD, D), jnp.bfloat16),
            pltpu.VMEM((2 * PAD, TOK), jnp.bfloat16),
            pltpu.VMEM((PAD, TOK), jnp.bfloat16),
            pltpu.VMEM(trio, jnp.bfloat16),
        ]
        + ([pltpu.VMEM(trio, jnp.bfloat16)] if blended else [])
        + [pltpu.VMEM(trio, firsts[0].dtype)] * 2
        + ([] if step else [pltpu.VMEM(trio, jnp.float32)] * 2)
        + [pltpu.SemaphoreType.DMA((2,)), pltpu.SemaphoreType.DMA],
        compiler_params=pltpu.CompilerParams(vmem_limit_bytes=32 * 2**20),
        cost_estimate=pl.CostEstimate(
            flops=2 * mults, bytes_accessed=16 * 2**20, transcendentals=ROWS * TOK
        ),
        name="adam_step",
    )(pos, fix, *args)
    return new[:3], new[3:6], new[6:9]


def shift_rep(value, hops):
    return lax.ppermute(value, "zl", [((i + hops) % 8, i) for i in range(8)])


def blend(mine, peer):
    return ((mine.astype(jnp.float32) + peer.astype(jnp.float32)) * 0.5).astype(jnp.bfloat16)


def z_partner(value):
    return lax.ppermute(value, "zh", [(0, 1), (1, 0)])


def ring_gather(value, x_core):
    groups = []
    for core in range(2):
        for k in range(4):
            if core == x_core:
                groups.append([i * 8 + core * 4 + k for i in range(4)])
            else:
                groups.append([k * 8 + core * 4 + i for i in range(4)])
    copies = jnp.broadcast_to(value[None], (4,) + value.shape)
    return lax.all_to_all(copies, ("x", "c", "y"), 0, 0, axis_index_groups=groups)


def core_swap(value):
    return lax.ppermute(value, "c", [(0, 1), (1, 0)])


def corrections(steps_done, step):
    count = (steps_done[0] + step + 1).astype(jnp.float32)
    fix_one = 1.0 - jnp.power(jnp.float32(beta_one), count)
    fix_two = 1.0 - jnp.power(jnp.float32(beta_two), count)
    return jnp.stack([rate / fix_one, 1.0 / fix_two])


def both_steps(power, steps_done, *arrays):
    hops = [2 ** ((power + s) % hop_levels) % 8 for s in range(STEPS)]
    weights = [a[0] for a in arrays[0:3]]
    firsts = [a[0] for a in arrays[3:6]]
    seconds = [a[0] for a in arrays[6:9]]
    inputs, cotangent = arrays[9:]
    pos = jnp.stack([lax.axis_index("c"), lax.axis_index("zh")]).astype(jnp.int32)
    own = [jnp.stack([inputs[s], cotangent[s]]) for s in range(STEPS)]
    other = [z_partner(v) for v in own]
    mine = ring_gather(ring_gather(jnp.stack((own[0], other[0])), 0), 1)
    mine, other[1] = lax.optimization_barrier((mine, other[1]))
    theirs = core_swap(mine)
    part = ring_gather(jnp.stack((own[1], other[1])), 0)
    theirs, part = lax.optimization_barrier((theirs, part))
    fix = corrections(steps_done, 0)
    weights, firsts, seconds = run_step(
        0, pos, fix, weights, None, firsts, seconds, (mine, theirs)
    )
    mine = ring_gather(part, 1)
    peers = None
    if hops[0]:
        peers = [shift_rep(w, hops[0]) for w in weights]
        mine, peers = lax.optimization_barrier((mine, peers))
    else:
        mine, weights = lax.optimization_barrier((mine, weights))
    theirs = core_swap(mine)
    fix = corrections(steps_done, 1)
    weights = run_step(1, pos, fix, weights, peers, firsts, seconds, (mine, theirs))[0]
    if hops[1]:
        weights = [blend(w, shift_rep(w, hops[1])) for w in weights]
    return tuple(w[None] for w in weights)


def local(steps_done, *arrays):
    branches = [
        lambda *operands, power=p: both_steps(power, *operands) for p in range(hop_levels)
    ]
    return lax.switch(steps_done[0] % hop_levels, branches, steps_done, *arrays)


def solution(mesh):
    fine = Mesh(mesh.devices.reshape(8, 4, 2, 2, 4), ("zl", "x", "c", "zh", "y"))
    rep, tp = ("zl", "x", "c"), ("zh", "y")
    weight = P(rep, tp, None)
    return jax.shard_map(
        local,
        mesh=fine,
        in_specs=(P(),) + (weight,) * 9 + (P(None, rep, tp),) * 2,
        out_specs=(weight,) * 3,
        check_vma=False,
    )
```

```python
import math

import jax
import jax.numpy as jnp
from jax import lax
from jax.experimental import pallas as pl
from jax.experimental.pallas import tpu as pltpu
from jax.sharding import Mesh, PartitionSpec as P

D = 2048
FF = 5632
STEPS = 2
ROWS = 88
LIMIT = 32
BLK = 256
TOKB = 128
TOK = 1024
NB = D // BLK

rate = 0.2
beta_one = 0.9
beta_two = 0.95
adam_eps = 1e-08
hop_levels = 5
INV_MODEL = 1.0 / math.sqrt(D)
INV_HIDDEN = 1.0 / math.sqrt(FF)


def dot(left, right, right_dim):
    return lax.dot_general(
        left, right, (((1,), (right_dim,)), ((), ())), preferred_element_type=jnp.float32
    )


def pad_rows(value):
    value = value.astype(jnp.float32)
    more = -value.shape[0] % 16
    if more:
        value = jnp.concatenate([value, jnp.zeros((more, value.shape[1]), jnp.float32)], 0)
    return value.astype(jnp.bfloat16)


def step_kernel(step, blended, part, pos, fix, *refs):
    low, rows = part
    pad = -(-rows // 16) * 16
    count = 1 if step else 3
    weights, refs = refs[:count], refs[count:]
    if blended:
        peers, refs = refs[0], refs[1:]
    firsts_in, seconds_in, refs = refs[:count], refs[count : 2 * count], refs[2 * count :]
    mine, theirs, refs = refs[0], refs[1], refs[2:]
    new_w, refs = refs[0], refs[1:]
    if not step:
        m_out, v_out, refs = refs[0], refs[1], refs[2:]
    gu_buf, v_buf, d_buf, h_buf, w_buf, refs = *refs[:5], refs[5:]
    if blended:
        p_buf, refs = refs[0], refs[1:]
    m_buf, s_buf, refs = refs[0], refs[1], refs[2:]
    if not step:
        new_m, new_v, refs = refs[0], refs[1], refs[2:]
    sem, out_sem = refs
    core, high = pos[0], pos[1]

    def block(x, y, z, kind):
        parts = []
        for half, source in enumerate((mine, theirs)):
            from_core = core if half == 0 else 1 - core
            near = jnp.where(from_core == 0, x, y)
            far = jnp.where(from_core == 0, y, x)
            parts.append(source[far, near, jnp.where(high == z, 0, 1), kind])
        return jnp.concatenate(parts, 0)

    def whole(sources, buf, which):
        if step:
            return [pltpu.make_async_copy(sources[0], buf, sem.at[which])]
        return [
            pltpu.make_async_copy(source, buf.at[i], sem.at[which])
            for i, source in enumerate(sources)
        ]

    tensors = whole(weights, w_buf, 0) + (whole([peers], p_buf, 0) if blended else [])
    moments = whole(firsts_in, m_buf, 1) + whole(seconds_in, s_buf, 1)
    for copy in tensors + moments:
        copy.start()
    for copy in tensors:
        copy.wait()

    def load(buf, i, cols):
        value = buf[i, :, cols].astype(jnp.float32)
        return value if step else value[low : low + rows]

    def weight(i, cols):
        mine = load(w_buf, i, cols)
        if blended:
            mine = (mine + load(p_buf, i, cols)) * 0.5
            mine = mine.astype(jnp.bfloat16).astype(jnp.float32)
        return mine

    def prepare(j, _):
        cols = pl.ds(pl.multiple_of(j * BLK, BLK), BLK)
        gu_buf[0:pad, cols] = pad_rows(weight(0, cols))
        gu_buf[pad : 2 * pad, cols] = pad_rows(weight(1, cols))
        v_buf[:, cols] = pad_rows(weight(2, cols))
        return 0

    lax.fori_loop(0, NB, prepare, 0)

    def forward(t, _):
        toks = pl.ds(pl.multiple_of(t * 256, 256), 256)
        gu = jnp.zeros((2 * pad, 256), jnp.float32)
        back = jnp.zeros((pad, 256), jnp.float32)
        for j in range(NB):
            cols = slice(j * BLK, (j + 1) * BLK)
            gu += dot(gu_buf[:, cols], block(t, j % 4, j // 4, 0), 1)
        for j in range(NB):
            cols = slice(j * BLK, (j + 1) * BLK)
            back += dot(v_buf[:, cols], block(t, j % 4, j // 4, 1), 1)
        gate, upper = gu[:pad] * INV_MODEL, gu[pad:] * INV_MODEL
        back = back * INV_HIDDEN
        sigma = jax.nn.sigmoid(gate)
        gs = gate * sigma
        h_buf[:, toks] = (gs * upper).astype(jnp.bfloat16)
        d_gate = back * upper * sigma * (1.0 + gate * (1.0 - sigma))
        d_buf[0:pad, toks] = d_gate.astype(jnp.bfloat16)
        d_buf[pad : 2 * pad, toks] = (back * gs).astype(jnp.bfloat16)
        return 0

    lax.fori_loop(0, TOK // 256, forward, 0)
    rate_one, inv_two = fix[0], fix[1]
    for copy in moments:
        copy.wait()

    def backward(j, _):
        cols = pl.ds(pl.multiple_of(j * BLK, BLK), BLK)
        y, z = j % 4, j // 4
        gu = jnp.zeros((2 * pad, BLK), jnp.float32)
        down = jnp.zeros((pad, BLK), jnp.float32)
        for x in range(4):
            toks = slice(x * 256, (x + 1) * 256)
            gu += dot(d_buf[:, toks], block(x, y, z, 0), 0)
            down += dot(h_buf[:, toks], block(x, y, z, 1), 0)
        grads = (gu[:rows], gu[pad : pad + rows], down[:rows])
        for i, grad in enumerate(grads):
            grad = grad * (INV_HIDDEN if i == 2 else INV_MODEL)
            first = beta_one * load(m_buf, i, cols) + (1.0 - beta_one) * grad
            second = beta_two * load(s_buf, i, cols) + (1.0 - beta_two) * grad * grad
            change = (first * rate_one) / (jnp.sqrt(second * inv_two) + adam_eps)
            new_w[i, :, cols] = (weight(i, cols) - change).astype(jnp.bfloat16)
            if not step:
                new_m[i, :, cols] = first
                new_v[i, :, cols] = second
                for buf, out in ((new_m, m_out), (new_v, v_out)):
                    pltpu.make_async_copy(
                        buf.at[i, :, cols], out.at[i, :, cols], out_sem
                    ).start()
        return 0

    lax.fori_loop(0, NB, backward, 0)
    if not step:
        for buf, out in ((new_m, m_out), (new_v, v_out)):
            pltpu.make_async_copy(buf, out, out_sem).wait()


def run_step(step, part, pos, fix, weights, peers, firsts, seconds, gathered):
    smem = pl.BlockSpec(memory_space=pltpu.SMEM)
    vmem = pl.BlockSpec(memory_space=pltpu.VMEM)
    hbm = pl.BlockSpec(memory_space=pltpu.HBM)
    blended = peers is not None
    rows = part[1]
    pad = -(-rows // 16) * 16
    args = [*weights, *([peers] if blended else []), *firsts, *seconds, *gathered]
    trio = (3, rows, D)
    held = trio if step else (3, ROWS, D)
    outs = [jax.ShapeDtypeStruct(trio, jnp.bfloat16)]
    if not step:
        outs += [jax.ShapeDtypeStruct(trio, jnp.float32)] * 2
    mults = 6 * rows * TOK * D

    def body(*refs):
        step_kernel(step, blended, part, *refs)

    return pl.pallas_call(
        body,
        out_shape=outs,
        in_specs=[smem, smem] + [hbm] * (len(args) - 2) + [vmem] * 2,
        out_specs=[vmem] + [hbm] * (len(outs) - 1),
        scratch_shapes=[
            pltpu.VMEM((2 * pad, D), jnp.bfloat16),
            pltpu.VMEM((pad, D), jnp.bfloat16),
            pltpu.VMEM((2 * pad, TOK), jnp.bfloat16),
            pltpu.VMEM((pad, TOK), jnp.bfloat16),
            pltpu.VMEM(held, jnp.bfloat16),
        ]
        + ([pltpu.VMEM(held, jnp.bfloat16)] if blended else [])
        + [pltpu.VMEM(held, firsts[0].dtype)] * 2
        + ([] if step else [pltpu.VMEM(trio, jnp.float32)] * 2)
        + [pltpu.SemaphoreType.DMA((2,)), pltpu.SemaphoreType.DMA],
        compiler_params=pltpu.CompilerParams(vmem_limit_bytes=LIMIT * 2**20),
        cost_estimate=pl.CostEstimate(
            flops=2 * mults, bytes_accessed=16 * 2**20, transcendentals=rows * TOK
        ),
        name="adam_step",
    )(pos, fix, *args)


def shift_rep(value, hops):
    return lax.ppermute(value, "zl", [((i + hops) % 8, i) for i in range(8)])


def blend(mine, peer):
    return ((mine.astype(jnp.float32) + peer.astype(jnp.float32)) * 0.5).astype(jnp.bfloat16)


def z_partner(value):
    return lax.ppermute(value, "zh", [(0, 1), (1, 0)])


def ring_gather(value, x_core):
    groups = []
    for core in range(2):
        for k in range(4):
            if core == x_core:
                groups.append([i * 8 + core * 4 + k for i in range(4)])
            else:
                groups.append([k * 8 + core * 4 + i for i in range(4)])
    copies = jnp.broadcast_to(value[None], (4,) + value.shape)
    return lax.all_to_all(copies, ("x", "c", "y"), 0, 0, axis_index_groups=groups)


def core_swap(value):
    return lax.ppermute(value, "c", [(0, 1), (1, 0)])


def corrections(steps_done, step):
    count = (steps_done[0] + step + 1).astype(jnp.float32)
    fix_one = 1.0 - jnp.power(jnp.float32(beta_one), count)
    fix_two = 1.0 - jnp.power(jnp.float32(beta_two), count)
    return jnp.stack([rate / fix_one, 1.0 / fix_two])


def both_steps(power, steps_done, *arrays):
    hops = [2 ** ((power + s) % hop_levels) % 8 for s in range(STEPS)]
    weights = [a[0] for a in arrays[0:3]]
    firsts = [a[0] for a in arrays[3:6]]
    seconds = [a[0] for a in arrays[6:9]]
    inputs, cotangent = arrays[9:]
    pos = jnp.stack([lax.axis_index("c"), lax.axis_index("zh")]).astype(jnp.int32)
    own = [jnp.stack([inputs[s], cotangent[s]]) for s in range(STEPS)]
    other = [z_partner(v) for v in own]
    mine = ring_gather(ring_gather(jnp.stack((own[0], other[0])), 0), 1)
    mine, other[1] = lax.optimization_barrier((mine, other[1]))
    theirs = core_swap(mine)
    part_one = ring_gather(jnp.stack((own[1], other[1])), 0)
    theirs, part_one = lax.optimization_barrier((theirs, part_one))
    parts = [(0, 48), (48, 40)] if any(hops) else [(0, ROWS)]
    fix = corrections(steps_done, 0)
    after = [
        run_step(0, part, pos, fix, weights, None, firsts, seconds, (mine, theirs))
        for part in parts
    ]
    mine = ring_gather(part_one, 1)
    peers = [None] * len(parts)
    if hops[0]:
        peers = [shift_rep(a[0], hops[0]) for a in after]
        peers[0], _ = lax.optimization_barrier((peers[0], after[-1][0]))
        mine, peers[0] = lax.optimization_barrier((mine, peers[0]))
    else:
        mine, after = lax.optimization_barrier((mine, after))
    theirs = core_swap(mine)
    fix = corrections(steps_done, 1)
    new = []
    for part, peer, (w, m, v) in zip(parts, peers, after):
        if new and hops[0]:
            peer, _ = lax.optimization_barrier((peer, new[-1]))
        new += run_step(1, part, pos, fix, [w], peer, [m], [v], (mine, theirs))
    if hops[1]:
        sent = list(new)
        if hops[0]:
            sent[0], _ = lax.optimization_barrier((new[0], peers[1]))
        others = [shift_rep(w, hops[1]) for w in sent]
        others[0], _ = lax.optimization_barrier((others[0], new[1]))
        first = blend(new[0], others[0])
        first, others[1] = lax.optimization_barrier((first, others[1]))
        new = [first, blend(new[1], others[1])]
    return tuple(jnp.concatenate([w[i] for w in new], 0)[None] for i in range(3))


def local(steps_done, *arrays):
    branches = [
        lambda *operands, power=p: both_steps(power, *operands) for p in range(hop_levels)
    ]
    return lax.switch(steps_done[0] % hop_levels, branches, steps_done, *arrays)


def solution(mesh):
    fine = Mesh(mesh.devices.reshape(8, 4, 2, 2, 4), ("zl", "x", "c", "zh", "y"))
    rep, tp = ("zl", "x", "c"), ("zh", "y")
    weight = P(rep, tp, None)
    return jax.shard_map(
        local,
        mesh=fine,
        in_specs=(P(),) + (weight,) * 9 + (P(None, rep, tp),) * 2,
        out_specs=(weight,) * 3,
        check_vma=False,
    )
```

```python
import math

import jax
import jax.numpy as jnp
from jax import lax
from jax.experimental import pallas as pl
from jax.experimental.pallas import tpu as pltpu
from jax.sharding import Mesh, PartitionSpec as P

D = 2048
FF = 5632
STEPS = 2
ROWS = 88
LIMIT = 32
BLK = 256
TOKB = 128
TOK = 1024
NB = D // BLK

rate = 0.2
beta_one = 0.9
beta_two = 0.95
adam_eps = 1e-08
hop_levels = 5
INV_MODEL = 1.0 / math.sqrt(D)
INV_HIDDEN = 1.0 / math.sqrt(FF)


def dot(left, right, right_dim):
    return lax.dot_general(
        left, right, (((1,), (right_dim,)), ((), ())), preferred_element_type=jnp.float32
    )


def pad_rows(value):
    value = value.astype(jnp.float32)
    more = -value.shape[0] % 16
    if more:
        value = jnp.concatenate([value, jnp.zeros((more, value.shape[1]), jnp.float32)], 0)
    return value.astype(jnp.bfloat16)


def step_kernel(step, blended, part, pos, fix, *refs):
    low, rows = part
    pad = -(-rows // 16) * 16
    count = 1 if step else 3
    weights, refs = refs[:count], refs[count:]
    if blended:
        peers, refs = refs[0], refs[1:]
    firsts_in, seconds_in, refs = refs[:count], refs[count : 2 * count], refs[2 * count :]
    mine, theirs, refs = refs[0], refs[1], refs[2:]
    new_w, refs = refs[0], refs[1:]
    if not step:
        m_out, v_out, refs = refs[0], refs[1], refs[2:]
    gu_buf, v_buf, d_buf, h_buf, refs = *refs[:4], refs[4:]
    m_buf, s_buf, refs = refs[0], refs[1], refs[2:]
    if not step:
        new_m, new_v, refs = refs[0], refs[1], refs[2:]
    sem, out_sem = refs
    core, high = pos[0], pos[1]

    def block(x, y, z, kind):
        parts = []
        for half, source in enumerate((mine, theirs)):
            from_core = core if half == 0 else 1 - core
            near = jnp.where(from_core == 0, x, y)
            far = jnp.where(from_core == 0, y, x)
            parts.append(source[far, near, jnp.where(high == z, 0, 1), kind])
        return jnp.concatenate(parts, 0)

    def whole(sources, buf):
        if step:
            return [pltpu.make_async_copy(sources[0], buf, sem)]
        return [
            pltpu.make_async_copy(source, buf.at[i], sem)
            for i, source in enumerate(sources)
        ]

    moments = whole(firsts_in, m_buf) + whole(seconds_in, s_buf)
    for copy in moments:
        copy.start()

    def load(buf, i, cols):
        value = buf[i, :, cols].astype(jnp.float32)
        return value if step else value[low : low + rows]

    def weight(i, cols):
        if not step:
            return weights[i][:, cols].astype(jnp.float32)[low : low + rows]
        mine = load(weights[0], i, cols)
        if blended:
            mine = (mine + load(peers, i, cols)) * 0.5
            mine = mine.astype(jnp.bfloat16).astype(jnp.float32)
        return mine

    def prepare(j, _):
        cols = pl.ds(pl.multiple_of(j * BLK, BLK), BLK)
        gu_buf[0:pad, cols] = pad_rows(weight(0, cols))
        gu_buf[pad : 2 * pad, cols] = pad_rows(weight(1, cols))
        v_buf[:, cols] = pad_rows(weight(2, cols))
        return 0

    lax.fori_loop(0, NB, prepare, 0)

    def forward(t, _):
        toks = pl.ds(pl.multiple_of(t * 256, 256), 256)
        gu = jnp.zeros((2 * pad, 256), jnp.float32)
        back = jnp.zeros((pad, 256), jnp.float32)
        for j in range(NB):
            cols = slice(j * BLK, (j + 1) * BLK)
            gu += dot(gu_buf[:, cols], block(t, j % 4, j // 4, 0), 1)
        for j in range(NB):
            cols = slice(j * BLK, (j + 1) * BLK)
            back += dot(v_buf[:, cols], block(t, j % 4, j // 4, 1), 1)
        gate, upper = gu[:pad] * INV_MODEL, gu[pad:] * INV_MODEL
        back = back * INV_HIDDEN
        sigma = jax.nn.sigmoid(gate)
        gs = gate * sigma
        h_buf[:, toks] = (gs * upper).astype(jnp.bfloat16)
        d_gate = back * upper * sigma * (1.0 + gate * (1.0 - sigma))
        d_buf[0:pad, toks] = d_gate.astype(jnp.bfloat16)
        d_buf[pad : 2 * pad, toks] = (back * gs).astype(jnp.bfloat16)
        return 0

    lax.fori_loop(0, TOK // 256, forward, 0)
    rate_one, inv_two = fix[0], fix[1]
    for copy in moments:
        copy.wait()

    def backward(j, _):
        cols = pl.ds(pl.multiple_of(j * BLK, BLK), BLK)
        y, z = j % 4, j // 4
        gu = jnp.zeros((2 * pad, BLK), jnp.float32)
        down = jnp.zeros((pad, BLK), jnp.float32)
        for x in range(4):
            toks = slice(x * 256, (x + 1) * 256)
            gu += dot(d_buf[:, toks], block(x, y, z, 0), 0)
            down += dot(h_buf[:, toks], block(x, y, z, 1), 0)
        grads = (gu[:rows], gu[pad : pad + rows], down[:rows])
        for i, grad in enumerate(grads):
            grad = grad * (INV_HIDDEN if i == 2 else INV_MODEL)
            first = beta_one * load(m_buf, i, cols) + (1.0 - beta_one) * grad
            second = beta_two * load(s_buf, i, cols) + (1.0 - beta_two) * grad * grad
            change = (first * rate_one) / (jnp.sqrt(second * inv_two) + adam_eps)
            new_w[i, :, cols] = (weight(i, cols) - change).astype(jnp.bfloat16)
            if not step:
                new_m[i, :, cols] = first
                new_v[i, :, cols] = second
                for buf, out in ((new_m, m_out), (new_v, v_out)):
                    pltpu.make_async_copy(
                        buf.at[i, :, cols], out.at[i, :, cols], out_sem
                    ).start()
        return 0

    lax.fori_loop(0, NB, backward, 0)
    if not step:
        for buf, out in ((new_m, m_out), (new_v, v_out)):
            pltpu.make_async_copy(buf, out, out_sem).wait()


def run_step(step, part, pos, fix, weights, peers, firsts, seconds, gathered):
    smem = pl.BlockSpec(memory_space=pltpu.SMEM)
    vmem = pl.BlockSpec(memory_space=pltpu.VMEM)
    hbm = pl.BlockSpec(memory_space=pltpu.HBM)
    blended = peers is not None
    rows = part[1]
    pad = -(-rows // 16) * 16
    direct = [*weights, *([peers] if blended else [])]
    moments = [*firsts, *seconds]
    trio = (3, rows, D)
    held = trio if step else (3, ROWS, D)
    outs = [jax.ShapeDtypeStruct(trio, jnp.bfloat16)]
    if not step:
        outs += [jax.ShapeDtypeStruct(trio, jnp.float32)] * 2
    mults = 6 * rows * TOK * D

    def body(*refs):
        step_kernel(step, blended, part, *refs)

    return pl.pallas_call(
        body,
        out_shape=outs,
        in_specs=[smem, smem] + [vmem] * len(direct) + [hbm] * len(moments) + [vmem] * 2,
        out_specs=[vmem] + [hbm] * (len(outs) - 1),
        scratch_shapes=[
            pltpu.VMEM((2 * pad, D), jnp.bfloat16),
            pltpu.VMEM((pad, D), jnp.bfloat16),
            pltpu.VMEM((2 * pad, TOK), jnp.bfloat16),
            pltpu.VMEM((pad, TOK), jnp.bfloat16),
        ]
        + [pltpu.VMEM(held, firsts[0].dtype)] * 2
        + ([] if step else [pltpu.VMEM(trio, jnp.float32)] * 2)
        + [pltpu.SemaphoreType.DMA] * 2,
        compiler_params=pltpu.CompilerParams(vmem_limit_bytes=LIMIT * 2**20),
        cost_estimate=pl.CostEstimate(
            flops=2 * mults, bytes_accessed=16 * 2**20, transcendentals=rows * TOK
        ),
        name="adam_step",
    )(pos, fix, *direct, *moments, *gathered)


def shift_rep(value, hops):
    return lax.ppermute(value, "zl", [((i + hops) % 8, i) for i in range(8)])


def blend(mine, peer):
    return ((mine.astype(jnp.float32) + peer.astype(jnp.float32)) * 0.5).astype(jnp.bfloat16)


def z_partner(value):
    return lax.ppermute(value, "zh", [(0, 1), (1, 0)])


def ring_gather(value, x_core):
    groups = []
    for core in range(2):
        for k in range(4):
            if core == x_core:
                groups.append([i * 8 + core * 4 + k for i in range(4)])
            else:
                groups.append([k * 8 + core * 4 + i for i in range(4)])
    copies = jnp.broadcast_to(value[None], (4,) + value.shape)
    return lax.all_to_all(copies, ("x", "c", "y"), 0, 0, axis_index_groups=groups)


def core_swap(value):
    return lax.ppermute(value, "c", [(0, 1), (1, 0)])


def corrections(steps_done, step):
    count = (steps_done[0] + step + 1).astype(jnp.float32)
    fix_one = 1.0 - jnp.power(jnp.float32(beta_one), count)
    fix_two = 1.0 - jnp.power(jnp.float32(beta_two), count)
    return jnp.stack([rate / fix_one, 1.0 / fix_two])


def both_steps(power, steps_done, *arrays):
    hops = [2 ** ((power + s) % hop_levels) % 8 for s in range(STEPS)]
    weights = [a[0] for a in arrays[0:3]]
    firsts = [a[0] for a in arrays[3:6]]
    seconds = [a[0] for a in arrays[6:9]]
    inputs, cotangent = arrays[9:]
    pos = jnp.stack([lax.axis_index("c"), lax.axis_index("zh")]).astype(jnp.int32)
    own = [jnp.stack([inputs[s], cotangent[s]]) for s in range(STEPS)]
    other = [z_partner(v) for v in own]
    mine = ring_gather(ring_gather(jnp.stack((own[0], other[0])), 0), 1)
    mine, other[1] = lax.optimization_barrier((mine, other[1]))
    theirs = core_swap(mine)
    part_one = ring_gather(jnp.stack((own[1], other[1])), 0)
    theirs, part_one = lax.optimization_barrier((theirs, part_one))
    parts = [(0, 48), (48, 40)] if any(hops) else [(0, ROWS)]
    fix = corrections(steps_done, 0)
    after = [
        run_step(0, part, pos, fix, weights, None, firsts, seconds, (mine, theirs))
        for part in parts
    ]
    mine = ring_gather(part_one, 1)
    peers = [None] * len(parts)
    if hops[0]:
        peers = [shift_rep(a[0], hops[0]) for a in after]
        peers[0], _ = lax.optimization_barrier((peers[0], after[-1][0]))
        mine, peers[0] = lax.optimization_barrier((mine, peers[0]))
    else:
        mine, after = lax.optimization_barrier((mine, after))
    theirs = core_swap(mine)
    fix = corrections(steps_done, 1)
    new = []
    for part, peer, (w, m, v) in zip(parts, peers, after):
        if new and hops[0]:
            peer, _ = lax.optimization_barrier((peer, new[-1]))
        new += run_step(1, part, pos, fix, [w], peer, [m], [v], (mine, theirs))
    if hops[1]:
        sent = list(new)
        if hops[0]:
            sent[0], _ = lax.optimization_barrier((new[0], peers[1]))
        others = [shift_rep(w, hops[1]) for w in sent]
        others[0], _ = lax.optimization_barrier((others[0], new[1]))
        first = blend(new[0], others[0])
        first, others[1] = lax.optimization_barrier((first, others[1]))
        new = [first, blend(new[1], others[1])]
    return tuple(jnp.concatenate([w[i] for w in new], 0)[None] for i in range(3))


def local(steps_done, *arrays):
    branches = [
        lambda *operands, power=p: both_steps(power, *operands) for p in range(hop_levels)
    ]
    return lax.switch(steps_done[0] % hop_levels, branches, steps_done, *arrays)


def solution(mesh):
    fine = Mesh(mesh.devices.reshape(8, 4, 2, 2, 4), ("zl", "x", "c", "zh", "y"))
    rep, tp = ("zl", "x", "c"), ("zh", "y")
    weight = P(rep, tp, None)
    return jax.shard_map(
        local,
        mesh=fine,
        in_specs=(P(),) + (weight,) * 9 + (P(None, rep, tp),) * 2,
        out_specs=(weight,) * 3,
        check_vma=False,
    )
```
